32 devices in a mesh: parts: 2 (over y), expert: 16 (over z, x, core), dp: 1.
Axes of the slice: x: 2, y: 2, z: 4, core: 2. Of those that a mesh axis runs over, the one named last changes fastest.
Arguments:
- tokens: bfloat16 [256, 4096], P(('parts', 'expert', 'dp')), parts along dimension 0, may hold values from -6 to 6
- relay: int32 [256], P(('parts', 'expert')), parts along dimension 0, may hold values from 0 to 7, as said below
- expert_ids: int32 [256, 8], P(('parts', 'expert')), parts along dimension 0, may hold values from 0 to 15, all different within a row; in each aligned block of 8 rows (0 to 7, 8 to 15, ...) at most 8 rows name the same one
- gates: bfloat16 [256, 8], P(('parts', 'expert')), parts along dimension 0, may hold values from 0.049804688 to 1
- w_gate: bfloat16 [16, 4096, 768], P('expert', None, 'dp'), may hold values from -0.09375 to 0.09375
- w_up: bfloat16 [16, 4096, 768], P('expert', None, 'dp'), may hold values from -0.09375 to 0.09375
- w_down: bfloat16 [16, 768, 4096], P('expert', 'dp'), may hold values from -0.21875 to 0.21875
Outputs:
- mixed: bfloat16 [256, 4096], P(('parts', 'expert'), 'dp'), parts along dimension 0
The draws below stay inside these ranges and needn't reach their ends.
There are 2 independent parts, one for each index of `parts`. The reference program is written for one: setup_inputs(seed, part) draws one part's arguments, and reference() takes and returns one part's arrays. A program takes and returns all parts, laid end to end along the dimension named above; an argument that names none is the same for every part. Nothing has to cross between parts.
Inputs may be any that keep to these rules, and one draw needn't show every extreme that they name: `relay`: each aligned block of 8 entries holds every number of 0 to 7 once. `expert_ids`: in each aligned block of 8 rows no expert is named by more than 8 rows, and in every draw some block has an expert named by exactly 8.
All inputs are finite; a program needn't handle non-finite values.
Results may differ from the reference program's by a relative error of at most 0.0049.
Values may be sent and summed in bfloat16 or wider, within the bound.
A program may use at most 128 MiB of HBM per device.

```python
import math
import jax
import jax.numpy as jnp
import numpy as np
from jax import lax

D = 4096
FF = 768
TOP = 8
ROW_DEV = 8
EXPERTS = 16
ROWS = 128
MOST = 8
CAP = 128
N_DP = 1


def draw_relay(key, part):
    key = jax.random.fold_in(key, 7)
    block = ROW_DEV * N_DP
    keys = jax.random.split(key, ROWS // block)
    perms = jax.vmap(lambda single: jax.random.permutation(single, block))(keys)
    return perms.reshape(ROWS).astype(jnp.int32)


def steps_of(own_key, extent, cuts, least, top_value):
    level, own = 1.0, jax.random.fold_in(own_key, 6)
    for dim, parts in cuts:
        draws = jnp.exp(jax.random.uniform(jax.random.fold_in(own, dim), (parts,), jnp.float32, least / len(cuts), top_value / len(cuts)))
        level = level * jnp.repeat(draws, extent[dim] // parts).reshape([-1 if axis == dim else 1 for axis in range(len(extent))])
    return level


def assign_block(stream_key, own, number, rows, number_of, top, bound, skew):
    sequence = jax.random.permutation(stream_key, number_of)
    crowded, common = shares(number_of, rows * top, bound, skew, True), shares(number_of, rows * top, bound, skew, False)
    places = jnp.arange(number_of)

    def named(sizes, turn):
        used = int((sizes > 0).sum())
        fixed = max(1, used // 4)
        passed = fixed + (places - fixed + turn * (used - fixed)) % max(1, number_of - fixed)
        return jnp.zeros((number_of,), jnp.int32).at[sequence[jnp.where(places < fixed, places, passed)]].set(jnp.asarray(sizes, jnp.int32))

    sizes = jnp.where(number % 4 == 0, named(crowded, number // 4), named(common, number - number // 4 - 1))
    mixed = jax.random.permutation(jax.random.fold_in(own, 3), number_of)
    donor, taker = mixed[0:number_of // 2 * 2:2], mixed[1:number_of // 2 * 2:2]
    room = jnp.minimum(sizes[donor] - 1, bound - sizes[taker]) // 2
    room = jnp.where((donor == sequence[0]) | (taker == sequence[0]) | (sizes[taker] == 0), 0, jnp.maximum(room, 0))
    passed = jax.random.randint(jax.random.fold_in(own, 4), (number_of // 2,), 0, 1 << 20) % (room + 1)
    sizes = sizes.at[donor].add(-passed).at[taker].add(passed)
    labels = jnp.searchsorted(jnp.cumsum(sizes), jnp.arange(rows * top), side="right").astype(jnp.int32)
    listing = labels.reshape(top, rows).T
    listing = listing[jax.random.permutation(jax.random.fold_in(own, 1), rows)]
    turn = jax.random.randint(jax.random.fold_in(own, 2), (rows, 1), 0, top)
    return jnp.take_along_axis(listing, (jnp.arange(top)[None, :] + turn) % top, axis=1)


def shares(number_of, total, most, lean, full):
    weights = [(1 << 20) // math.isqrt(grade ** lean) + 1 for grade in range(1, number_of + 1)]
    largest = most if full else min(most, max(-(-total // number_of), total * weights[0] // sum(weights)))
    least = 1 if total - largest >= number_of - 1 else 0
    given, spare = [largest] + [least] * (number_of - 1), total - largest - least * (number_of - 1)
    while spare > 0:
        movable = [i for i in range(1, number_of) if given[i] < largest] or [i for i in range(1, number_of) if given[i] < most]
        pool, left = sum([weights[i] for i in movable]), spare
        for i in movable:
            more = min(most - given[i], max(1, left * weights[i] // pool), spare)
            given[i] = given[i] + more
            spare = spare - more
    return np.array(given)


def gaussian(own_key, dims, spread, most, shards=(), held_as=jnp.bfloat16):
    result = spread * jax.random.normal(own_key, dims, jnp.float32)
    if shards:
        result = result * steps_of(own_key, dims, shards, -0.22, 0.18)
    return jnp.clip(result, -most, most).astype(held_as)


def setup_inputs(seed: int = 0, part: int = 0) -> dict:
    key_of = jax.random.split(jax.random.key(seed), 8)
    part_splits = jax.random.split(jax.random.fold_in(key_of[7], part), 8)
    tokens = gaussian(part_splits[0], (ROWS, D), 1.0, 6.0, ((0, 16),))
    relay = draw_relay(jax.random.fold_in(jax.random.fold_in(key_of[7], part), 71), part)
    expert_ids_keys = jax.random.split(jax.random.fold_in(part_splits[2], 1), ROWS // (ROW_DEV * N_DP))
    expert_ids_turns = jax.random.permutation(jax.random.fold_in(part_splits[2], 3), ROWS // (ROW_DEV * N_DP))
    expert_ids = jax.vmap(lambda own, number: assign_block(jax.random.fold_in(part_splits[2], 2), own, number, ROW_DEV * N_DP, EXPERTS, TOP, MOST, 2))(expert_ids_keys, expert_ids_turns).reshape((ROWS, TOP))
    gates = jnp.clip(0.049804688 + 0.9501953 * jax.random.uniform(part_splits[3], (ROWS, TOP), jnp.float32) ** steps_of(part_splits[3], (ROWS, TOP), ((0, 16),), -0.2, 0.2), 0.049804688, 1.0).astype(jnp.bfloat16)
    w_gate = gaussian(key_of[4], (EXPERTS, D, FF), D ** -0.5, 0.09375, ((0, 16),))
    w_up = gaussian(key_of[5], (EXPERTS, D, FF), D ** -0.5, 0.09375, ((0, 16),))
    w_down = gaussian(key_of[6], (EXPERTS, FF, D), FF ** -0.5, 0.21875, ((0, 16),))
    return dict(tokens=tokens, relay=relay, expert_ids=expert_ids, gates=gates, w_gate=w_gate, w_up=w_up, w_down=w_down)


def reference(tokens, relay, expert_ids, gates, w_gate, w_up, w_down):
    block = ROW_DEV * N_DP
    base = (jnp.arange(ROWS, dtype=jnp.int32) // block) * block
    moe_rows = tokens[(base + relay).astype(jnp.int32)]
    gate_f = gates.astype(jnp.float32)

    def one_expert(total, index):
        hit = expert_ids == index
        marked = jnp.any(hit, axis=1).astype(jnp.int32)
        weight = jnp.sum(jnp.where(hit, gate_f, jnp.zeros_like(gate_f)), axis=1)
        order = jnp.argsort(1 - marked, stable=True)[:CAP].astype(jnp.int32)
        picked = moe_rows[order]
        gate_val = jnp.dot(picked, w_gate[index], preferred_element_type=jnp.float32)
        up_val = jnp.dot(picked, w_up[index], preferred_element_type=jnp.float32)
        hidden = (jax.nn.silu(gate_val) * up_val).astype(jnp.bfloat16)
        output = jnp.dot(hidden, w_down[index], preferred_element_type=jnp.float32)
        scale = weight[order] * marked[order].astype(weight.dtype)
        return total.at[order].add(output * scale[:, None]), None

    start = jnp.zeros((ROWS, D), jnp.float32)
    total, unused = lax.scan(one_expert, start, jnp.arange(EXPERTS, dtype=jnp.int32))
    return total.astype(jnp.bfloat16)
```

```python
import functools

import jax
import jax.numpy as jnp
from jax import lax
from jax.experimental import pallas as pl
from jax.experimental.pallas import tpu as pltpu
from jax.sharding import PartitionSpec as P


def slot_limit(block, top, experts):
    return min(block, max(2, 2 * block * top // experts))


def expert_part(moe_all, ids_all, gates_all, w_gate, w_up, w_down, block):
    rows = moe_all.shape[0]
    experts = lax.axis_size("expert")
    top = ids_all.shape[1]
    capacity = min(rows, slot_limit(block, top, experts) * experts)
    index = lax.axis_index("expert")
    hit = ids_all == index
    gate_f = gates_all.astype(jnp.float32)
    marked = jnp.any(hit, axis=1).astype(jnp.int32)
    weight = jnp.sum(jnp.where(hit, gate_f, jnp.zeros_like(gate_f)), axis=1)
    order = jnp.argsort(1 - marked, stable=True)[:capacity]
    picked = moe_all[order]
    gate_val = jnp.dot(picked, w_gate[0], preferred_element_type=jnp.float32)
    up_val = jnp.dot(picked, w_up[0], preferred_element_type=jnp.float32)
    hidden = (jax.nn.silu(gate_val) * up_val).astype(jnp.bfloat16)
    output = jnp.dot(hidden, w_down[0], preferred_element_type=jnp.float32)
    valid = marked[order]
    scale = weight[order] * valid.astype(jnp.float32)
    return (order, valid, marked, output * scale[:, None])


def body(tokens, relay, expert_ids, gates, w_gate, w_up, w_down):
    side = lax.axis_index("dp")
    block = relay.shape[0]
    block_rows = lax.all_gather(tokens, "dp", axis=0, tiled=True)
    local_rows = block_rows[relay]
    moe_all, ids_all, gates_all = (
        lax.all_gather(local_rows, "expert", axis=0, tiled=True),
        lax.all_gather(expert_ids, "expert", axis=0, tiled=True),
        lax.all_gather(gates, "expert", axis=0, tiled=True),
    )
    order, valid, marked, scaled = expert_part(
        moe_all, ids_all, gates_all, w_gate, w_up, w_down, block
    )
    rows = moe_all.shape[0]
    width = tokens.shape[1] // lax.axis_size("dp")
    partial_sum = jnp.zeros((rows, moe_all.shape[1]), jnp.float32).at[order].add(scaled)
    total = lax.psum(partial_sum, ("expert", "dp"))
    row_start = lax.axis_index("expert") * block
    col_start = side * width
    result = lax.dynamic_slice(total, (row_start, col_start), (block, width))
    return result.astype(jnp.bfloat16)


KC = 4
NC = 4
LANES = 128


def fused_kernel(nz, relay_ref, tok_ref, ids_ref, gates_ref, wg_hbm, wu_hbm, wd_hbm, out_ref,
                 wg, wu, wd, acc_g, acc_u, g_bufs, f_bufs, c_out, c_in, x_out, x_in, z_out, z_in,
                 w_sem, zs, zr, xs, xr, cs, cr, rcs, rcr, rxs, rxr, rzs, rzr):
    f32, bf16 = jnp.float32, jnp.bfloat16
    rows, d = tok_ref.shape
    ff = wg.shape[1]
    total = 4 * nz * rows
    kw, nw = d // KC, d // NC
    me = lax.axis_index("expert")
    c, x, z = lax.rem(me, 2), lax.rem(me // 2, 2), me // 4
    oc, ox = 1 - c, 1 - x

    def dev(zz, xx, cc):
        return {"expert": zz * 4 + xx * 2 + cc}

    w_copies = []
    for k in range(KC):
        part = pl.ds(k * kw, kw)
        w_copies.append((
            pltpu.make_async_copy(wg_hbm.at[0, part], wg.at[part], w_sem.at[0, k]),
            pltpu.make_async_copy(wu_hbm.at[0, part], wu.at[part], w_sem.at[1, k]),
        ))
    d_copies = [
        pltpu.make_async_copy(wd_hbm.at[0, :, pl.ds(j * nw, nw)], wd.at[j], w_sem.at[2, j])
        for j in range(NC)
    ]
    for pair in w_copies:
        for copy in pair:
            copy.start()
    for copy in d_copies:
        copy.start()

    zto = [lax.rem(z + s, nz) for s in range(1, nz)]
    zfrom = [lax.rem(z + nz - s, nz) for s in range(1, nz)]
    barrier = pltpu.get_barrier_semaphore()
    partners = [dev(z, x, oc), dev(z, ox, c)] + [dev(t, x, c) for t in zto]
    for partner in partners:
        pl.semaphore_signal(barrier, inc=1, device_id=partner, device_id_type=pl.DeviceIdType.MESH)

    sub = lax.broadcasted_iota(jnp.int32, (rows, rows), 0)
    lane = lax.broadcasted_iota(jnp.int32, (rows, rows), 1)
    source = jnp.zeros((rows, rows), jnp.int32)
    for r in range(rows):
        source = jnp.where(sub == r, relay_ref[r], source)
    pick = jnp.where(source == lane, 1.0, 0.0).astype(bf16)
    wide = lax.broadcasted_iota(jnp.int32, (rows, LANES), 1)
    dense = jnp.zeros((rows, LANES), f32)
    ids = ids_ref[...]
    gates = gates_ref[...].astype(f32)
    for t in range(ids_ref.shape[1]):
        dense = dense + jnp.where(ids[:, t:t + 1] == wide, gates[:, t:t + 1], 0.0)
    for k in range(KC):
        moved = jnp.dot(pick, tok_ref[:, k * kw:(k + 1) * kw], preferred_element_type=f32)
        g_bufs[k][c, x, z, :, 0:kw] = moved.astype(bf16)
    g_bufs[0][c, x, z, :, kw:kw + LANES] = dense.astype(bf16)

    pl.semaphore_wait(barrier, len(partners))

    sent = []

    def send(src, dst, ss, rs, to):
        copy = pltpu.make_async_remote_copy(
            src_ref=src, dst_ref=dst, send_sem=ss, recv_sem=rs,
            device_id=to, device_id_type=pl.DeviceIdType.MESH)
        copy.start()
        sent.append(copy)

    def arrived(dst, ss, rs, to):
        pltpu.make_async_remote_copy(
            src_ref=dst, dst_ref=dst, send_sem=ss, recv_sem=rs,
            device_id=to, device_id_type=pl.DeviceIdType.MESH).wait_recv()

    sib, beside = dev(z, x, oc), dev(z, ox, c)

    for k in range(KC):
        for s in range(nz - 1):
            send(g_bufs[k].at[c, x, z], g_bufs[k].at[c, x, z], zs.at[k, s], zr.at[k, s], dev(zto[s], x, c))

    def in_z(k):
        g = g_bufs[k]
        for s in range(nz - 1):
            arrived(g.at[c, x, zfrom[s]], zs.at[k, s], zr.at[k, s], dev(zto[s], x, c))
        send(g.at[c, x], g.at[c, x], xs.at[k], xr.at[k], beside)
        send(g.at[c, x], g.at[c, x], cs.at[k, 0], cr.at[k, 0], sib)

    def in_x(k):
        g = g_bufs[k]
        arrived(g.at[c, ox], xs.at[k], xr.at[k], beside)
        send(g.at[c, ox], g.at[c, ox], cs.at[k, 1], cr.at[k, 1], sib)

    def multiply(k):
        g = g_bufs[k]
        arrived(g.at[oc, x], cs.at[k, 0], cr.at[k, 0], sib)
        arrived(g.at[oc, ox], cs.at[k, 1], cr.at[k, 1], sib)
        a = g[:, :, :, :, 0:kw].reshape(total, kw)
        for copy, w, acc in zip(w_copies[k], (wg, wu), (acc_g, acc_u)):
            copy.wait()
            part = jnp.dot(a, w[k * kw:(k + 1) * kw, :], preferred_element_type=f32)
            if k == 0:
                acc[...] = part
            else:
                acc[...] += part

    steps = []
    for k in range(KC + 2):
        if k < KC:
            in_z(k)
        if 0 <= k - 1 < KC:
            in_x(k - 1)
        if 0 <= k - 2 < KC:
            multiply(k - 2)

    weights = g_bufs[0][:, :, :, :, kw:kw + LANES].reshape(total, LANES).astype(f32)
    mine = lax.broadcasted_iota(jnp.int32, (total, LANES), 1) == me
    weight = jnp.sum(jnp.where(mine, weights, 0.0), axis=1, keepdims=True)
    gate = acc_g[...]
    hidden = (gate / (1.0 + jnp.exp(-gate)) * acc_u[...]).astype(bf16)

    def down(j):
        f = f_bufs[j]
        d_copies[j].wait()
        part = jnp.dot(hidden, wd[j], preferred_element_type=f32) * weight
        f[...] = part.reshape(2, 2, nz, rows, nw)
        c_out[j] = f[oc].astype(bf16)
        send(c_out.at[j], c_in.at[j], rcs.at[j], rcr.at[j], sib)

    def out_x(j):
        f = f_bufs[j]
        arrived(c_in.at[j], rcs.at[j], rcr.at[j], sib)
        x_out[j] = (f[c, ox] + c_in[j, ox].astype(f32)).astype(bf16)
        send(x_out.at[j], x_in.at[j], rxs.at[j], rxr.at[j], beside)

    def out_z(j):
        f = f_bufs[j]
        arrived(x_in.at[j], rxs.at[j], rxr.at[j], beside)
        t = f[c, x] + c_in[j, x].astype(f32) + x_in[j].astype(f32)
        f[c, x] = t
        z_out[j] = t.astype(bf16)
        for s in range(nz - 1):
            send(z_out.at[j, zto[s]], z_in.at[j, s], rzs.at[j, s], rzr.at[j, s], dev(zto[s], x, c))

    def finish(j):
        t = f_bufs[j][c, x, z]
        for s in range(nz - 1):
            arrived(z_in.at[j, s], rzs.at[j, s], rzr.at[j, s], dev(zto[s], x, c))
            t = t + z_in[j, s].astype(f32)
        out_ref[:, j * nw:(j + 1) * nw] = t.astype(bf16)

    for j in range(NC + 3):
        if j < NC:
            down(j)
        if 0 <= j - 1 < NC:
            out_x(j - 1)
        if 0 <= j - 2 < NC:
            out_z(j - 2)
        if 0 <= j - 3 < NC:
            finish(j - 3)

    for copy in sent:
        copy.wait_send()


def fused(experts, tokens, relay, expert_ids, gates, w_gate, w_up, w_down):
    rows, d = tokens.shape
    ff = w_gate.shape[2]
    nz = experts // 4
    kw, nw = d // KC, d // NC
    bf16, f32 = jnp.bfloat16, jnp.float32
    vmem = pl.BlockSpec(memory_space=pltpu.VMEM)
    hbm = pl.BlockSpec(memory_space=pl.ANY)
    dma = pltpu.SemaphoreType.DMA
    total = experts * rows
    return pl.pallas_call(
        functools.partial(fused_kernel, nz),
        out_shape=jax.ShapeDtypeStruct((rows, d), bf16),
        in_specs=[pl.BlockSpec(memory_space=pltpu.SMEM), vmem, vmem, vmem, hbm, hbm, hbm],
        out_specs=vmem,
        scratch_shapes=[
            pltpu.VMEM((d, ff), bf16),
            pltpu.VMEM((d, ff), bf16),
            pltpu.VMEM((NC, ff, nw), bf16),
            pltpu.VMEM((total, ff), f32),
            pltpu.VMEM((total, ff), f32),
            [pltpu.VMEM((2, 2, nz, rows, kw + (LANES if k == 0 else 0)), bf16) for k in range(KC)],
            [pltpu.VMEM((2, 2, nz, rows, nw), f32) for j in range(NC)],
            pltpu.VMEM((NC, 2, nz, rows, nw), bf16),
            pltpu.VMEM((NC, 2, nz, rows, nw), bf16),
            pltpu.VMEM((NC, nz, rows, nw), bf16),
            pltpu.VMEM((NC, nz, rows, nw), bf16),
            pltpu.VMEM((NC, nz, rows, nw), bf16),
            pltpu.VMEM((NC, nz - 1, rows, nw), bf16),
            dma((3, max(KC, NC))),
            dma((KC, nz - 1)), dma((KC, nz - 1)),
            dma((KC,)), dma((KC,)),
            dma((KC, 2)), dma((KC, 2)),
            dma((NC,)), dma((NC,)),
            dma((NC,)), dma((NC,)),
            dma((NC, nz - 1)), dma((NC, nz - 1)),
        ],
        compiler_params=pltpu.CompilerParams(
            collective_id=0, has_side_effects=True, vmem_limit_bytes=56 * 1024 * 1024),
        cost_estimate=pl.CostEstimate(
            flops=6 * total * d * ff, bytes_accessed=6 * d * ff, transcendentals=total * ff),
    )(relay, tokens, expert_ids, gates, w_gate, w_up, w_down)


def solution(mesh):
    experts = mesh.shape["expert"]
    fits = mesh.shape["dp"] == 1 and experts == 16
    return jax.shard_map(
        functools.partial(fused, experts) if fits else body,
        mesh=mesh,
        in_specs=(
            P(("parts", "expert", "dp"), None),
            P(("parts", "expert")),
            P(("parts", "expert"), None),
            P(("parts", "expert"), None),
            P("expert", None, "dp"),
            P("expert", None, "dp"),
            P("expert", "dp", None),
        ),
        out_specs=P(("parts", "expert"), "dp"),
        check_vma=False,
    )
```

```python
import functools

import jax
import jax.numpy as jnp
from jax import lax
from jax.experimental import pallas as pl
from jax.experimental.pallas import tpu as pltpu
from jax.sharding import PartitionSpec as P


def slot_limit(block, top, experts):
    return min(block, max(2, 2 * block * top // experts))


def expert_part(moe_all, ids_all, gates_all, w_gate, w_up, w_down, block):
    rows = moe_all.shape[0]
    experts = lax.axis_size("expert")
    top = ids_all.shape[1]
    capacity = min(rows, slot_limit(block, top, experts) * experts)
    index = lax.axis_index("expert")
    hit = ids_all == index
    gate_f = gates_all.astype(jnp.float32)
    marked = jnp.any(hit, axis=1).astype(jnp.int32)
    weight = jnp.sum(jnp.where(hit, gate_f, jnp.zeros_like(gate_f)), axis=1)
    order = jnp.argsort(1 - marked, stable=True)[:capacity]
    picked = moe_all[order]
    gate_val = jnp.dot(picked, w_gate[0], preferred_element_type=jnp.float32)
    up_val = jnp.dot(picked, w_up[0], preferred_element_type=jnp.float32)
    hidden = (jax.nn.silu(gate_val) * up_val).astype(jnp.bfloat16)
    output = jnp.dot(hidden, w_down[0], preferred_element_type=jnp.float32)
    valid = marked[order]
    scale = weight[order] * valid.astype(jnp.float32)
    return (order, valid, marked, output * scale[:, None])


def body(tokens, relay, expert_ids, gates, w_gate, w_up, w_down):
    side = lax.axis_index("dp")
    block = relay.shape[0]
    block_rows = lax.all_gather(tokens, "dp", axis=0, tiled=True)
    local_rows = block_rows[relay]
    moe_all, ids_all, gates_all = (
        lax.all_gather(local_rows, "expert", axis=0, tiled=True),
        lax.all_gather(expert_ids, "expert", axis=0, tiled=True),
        lax.all_gather(gates, "expert", axis=0, tiled=True),
    )
    order, valid, marked, scaled = expert_part(
        moe_all, ids_all, gates_all, w_gate, w_up, w_down, block
    )
    rows = moe_all.shape[0]
    width = tokens.shape[1] // lax.axis_size("dp")
    partial_sum = jnp.zeros((rows, moe_all.shape[1]), jnp.float32).at[order].add(scaled)
    total = lax.psum(partial_sum, ("expert", "dp"))
    row_start = lax.axis_index("expert") * block
    col_start = side * width
    result = lax.dynamic_slice(total, (row_start, col_start), (block, width))
    return result.astype(jnp.bfloat16)


KC = 2
NC = 2
LANES = 128


def fused_kernel(relay_ref, tok_ref, ids_ref, gates_ref, wg_hbm, wu_hbm, wd_hbm, out_ref,
                 wg, wu, wd, acc_g, acc_u, g_bufs, f_bufs, c_out, c_in, x_out, x_in, z_out, z_in,
                 w_sem, zs, zr, xs, xr, cs, cr, rcs, rcr, rxs, rxr, rzs, rzr):
    f32, bf16 = jnp.float32, jnp.bfloat16
    rows, d = tok_ref.shape
    ff = wg.shape[1]
    total = 16 * rows
    kw, nw = d // KC, d // NC
    me = lax.axis_index("expert")
    c, x, z = lax.rem(me, 2), lax.rem(me // 2, 2), me // 4
    oc, ox = 1 - c, 1 - x

    def dev(zz, xx, cc):
        return {"expert": zz * 4 + xx * 2 + cc}

    w_copies = []
    for k in range(KC):
        part = pl.ds(k * kw, kw)
        w_copies.append((
            pltpu.make_async_copy(wg_hbm.at[0, part], wg.at[part], w_sem.at[0, k]),
            pltpu.make_async_copy(wu_hbm.at[0, part], wu.at[part], w_sem.at[1, k]),
        ))
    d_copies = [
        pltpu.make_async_copy(wd_hbm.at[0, :, pl.ds(j * nw, nw)], wd.at[j], w_sem.at[2, j])
        for j in range(NC)
    ]
    for pair in w_copies:
        for copy in pair:
            copy.start()
    for copy in d_copies:
        copy.start()

    h, l = z // 2, lax.rem(z, 2)
    oh, ol = 1 - h, 1 - l
    sib, mirror = dev(z, x, oc), dev(3 - z, x, c)
    spots = ((x, ol), (ox, l), (ox, ol))
    near = [dev(2 * h + ll, xx, c) for xx, ll in spots]
    barrier = pltpu.get_barrier_semaphore()
    partners = [sib, mirror] + near
    for partner in partners:
        pl.semaphore_signal(barrier, inc=1, device_id=partner, device_id_type=pl.DeviceIdType.MESH)

    sub = lax.broadcasted_iota(jnp.int32, (rows, rows), 0)
    lane = lax.broadcasted_iota(jnp.int32, (rows, rows), 1)
    source = jnp.zeros((rows, rows), jnp.int32)
    for r in range(rows):
        source = jnp.where(sub == r, relay_ref[r], source)
    pick = jnp.where(source == lane, 1.0, 0.0).astype(bf16)
    wide = lax.broadcasted_iota(jnp.int32, (rows, LANES), 1)
    dense = jnp.zeros((rows, LANES), f32)
    ids = ids_ref[...]
    gates = gates_ref[...].astype(f32)
    for t in range(ids_ref.shape[1]):
        dense = dense + jnp.where(ids[:, t:t + 1] == wide, gates[:, t:t + 1], 0.0)
    for k in range(KC):
        moved = jnp.dot(pick, tok_ref[:, k * kw:(k + 1) * kw], preferred_element_type=f32)
        g_bufs[k][c, h, x, l, :, 0:kw] = moved.astype(bf16)
    g_bufs[0][c, h, x, l, :, kw:kw + LANES] = dense.astype(bf16)

    pl.semaphore_wait(barrier, len(partners))

    sent = []

    def send(src, dst, ss, rs, to):
        copy = pltpu.make_async_remote_copy(
            src_ref=src, dst_ref=dst, send_sem=ss, recv_sem=rs,
            device_id=to, device_id_type=pl.DeviceIdType.MESH)
        copy.start()
        sent.append(copy)

    def arrived(dst, ss, rs, to):
        pltpu.make_async_remote_copy(
            src_ref=dst, dst_ref=dst, send_sem=ss, recv_sem=rs,
            device_id=to, device_id_type=pl.DeviceIdType.MESH).wait_recv()

    def begin_far(k):
        block = g_bufs[k].at[c, h, x, l]
        send(block, block, zs.at[k, 3], zr.at[k, 3], mirror)

    def begin_near(k):
        block = g_bufs[k].at[c, h, x, l]
        for p in range(3):
            send(block, block, zs.at[k, p], zr.at[k, p], near[p])

    def forward(k):
        block = g_bufs[k].at[c, oh, x, ol]
        arrived(block, zs.at[k, 3], zr.at[k, 3], mirror)
        for p in range(3):
            send(block, block, xs.at[k, p], xr.at[k, p], near[p])

    def share_near(k):
        g = g_bufs[k]
        for p, (xx, ll) in enumerate(spots):
            arrived(g.at[c, h, xx, ll], zs.at[k, p], zr.at[k, p], near[p])
        send(g.at[c, h], g.at[c, h], cs.at[k, 0], cr.at[k, 0], sib)

    def share_far(k):
        g = g_bufs[k]
        for p, (xx, ll) in enumerate(spots):
            arrived(g.at[c, oh, xx, 1 - ll], xs.at[k, p], xr.at[k, p], near[p])
        send(g.at[c, oh], g.at[c, oh], cs.at[k, 1], cr.at[k, 1], sib)

    def multiply(k):
        g = g_bufs[k]
        arrived(g.at[oc, h], cs.at[k, 0], cr.at[k, 0], sib)
        arrived(g.at[oc, oh], cs.at[k, 1], cr.at[k, 1], sib)
        a = g[:, :, :, :, :, 0:kw].reshape(total, kw)
        for copy, w, acc in zip(w_copies[k], (wg, wu), (acc_g, acc_u)):
            copy.wait()
            part = jnp.dot(a, w[k * kw:(k + 1) * kw, :], preferred_element_type=f32)
            if k == 0:
                acc[...] = part
            else:
                acc[...] += part

    for k in range(KC):
        begin_far(k)
    for k in range(KC):
        begin_near(k)
    for k in range(KC):
        forward(k)
        share_near(k)
    for k in range(KC):
        share_far(k)
        multiply(k)

    weights = g_bufs[0][:, :, :, :, :, kw:kw + LANES].reshape(total, LANES).astype(f32)
    mine = lax.broadcasted_iota(jnp.int32, (total, LANES), 1) == me
    weight = jnp.sum(jnp.where(mine, weights, 0.0), axis=1, keepdims=True)
    gate = acc_g[...]
    hidden = (gate / (1.0 + jnp.exp(-gate)) * acc_u[...]).astype(bf16)

    def down(j):
        f = f_bufs[j]
        d_copies[j].wait()
        part = jnp.dot(hidden, wd[j], preferred_element_type=f32) * weight
        f[...] = part.reshape(f.shape)
        for q, hh in enumerate((oh, h)):
            c_out[j, hh] = f[oc, hh].astype(bf16)
            send(c_out.at[j, hh], c_in.at[j, hh], rcs.at[j, q], rcr.at[j, q], sib)

    def both(j, hh, xx, ll):
        return f_bufs[j][c, hh, xx, ll] + c_in[j, hh, xx, ll].astype(f32)

    def out_far(j):
        arrived(c_in.at[j, oh], rcs.at[j, 0], rcr.at[j, 0], sib)
        for p, (xx, ll) in enumerate(spots):
            x_out[j, p] = both(j, oh, xx, 1 - ll).astype(bf16)
            send(x_out.at[j, p], x_in.at[j, p], rxs.at[j, p], rxr.at[j, p], near[p])

    def out_near(j):
        arrived(c_in.at[j, h], rcs.at[j, 1], rcr.at[j, 1], sib)
        for p, (xx, ll) in enumerate(spots):
            z_out[j, p] = both(j, h, xx, ll).astype(bf16)
            send(z_out.at[j, p], z_in.at[j, p], rzs.at[j, p], rzr.at[j, p], near[p])

    def cross(j):
        t = both(j, oh, x, ol)
        for p in range(3):
            arrived(x_in.at[j, p], rxs.at[j, p], rxr.at[j, p], near[p])
            t = t + x_in[j, p].astype(f32)
        x_out[j, 3] = t.astype(bf16)
        send(x_out.at[j, 3], x_in.at[j, 3], rxs.at[j, 3], rxr.at[j, 3], mirror)

    def finish(j):
        t = both(j, h, x, l)
        for p in range(3):
            arrived(z_in.at[j, p], rzs.at[j, p], rzr.at[j, p], near[p])
            t = t + z_in[j, p].astype(f32)
        arrived(x_in.at[j, 3], rxs.at[j, 3], rxr.at[j, 3], mirror)
        t = t + x_in[j, 3].astype(f32)
        out_ref[:, j * nw:(j + 1) * nw] = t.astype(bf16)

    for j in range(NC):
        down(j)
        out_far(j)
    for j in range(NC):
        out_near(j)
        cross(j)
    for j in range(NC):
        finish(j)

    for copy in sent:
        copy.wait_send()


def fused(experts, tokens, relay, expert_ids, gates, w_gate, w_up, w_down):
    rows, d = tokens.shape
    ff = w_gate.shape[2]
    kw, nw = d // KC, d // NC
    bf16, f32 = jnp.bfloat16, jnp.float32
    vmem = pl.BlockSpec(memory_space=pltpu.VMEM)
    hbm = pl.BlockSpec(memory_space=pl.ANY)
    dma = pltpu.SemaphoreType.DMA
    total = experts * rows
    return pl.pallas_call(
        fused_kernel,
        out_shape=jax.ShapeDtypeStruct((rows, d), bf16),
        in_specs=[pl.BlockSpec(memory_space=pltpu.SMEM), vmem, vmem, vmem, hbm, hbm, hbm],
        out_specs=vmem,
        scratch_shapes=[
            pltpu.VMEM((d, ff), bf16),
            pltpu.VMEM((d, ff), bf16),
            pltpu.VMEM((NC, ff, nw), bf16),
            pltpu.VMEM((total, ff), f32),
            pltpu.VMEM((total, ff), f32),
            [pltpu.VMEM((2, 2, 2, 2, rows, kw + (LANES if k == 0 else 0)), bf16) for k in range(KC)],
            [pltpu.VMEM((2, 2, 2, 2, rows, nw), f32) for j in range(NC)],
            pltpu.VMEM((NC, 2, 2, 2, rows, nw), bf16),
            pltpu.VMEM((NC, 2, 2, 2, rows, nw), bf16),
            pltpu.VMEM((NC, 4, rows, nw), bf16),
            pltpu.VMEM((NC, 4, rows, nw), bf16),
            pltpu.VMEM((NC, 3, rows, nw), bf16),
            pltpu.VMEM((NC, 3, rows, nw), bf16),
            dma((3, max(KC, NC))),
            dma((KC, 4)), dma((KC, 4)),
            dma((KC, 3)), dma((KC, 3)),
            dma((KC, 2)), dma((KC, 2)),
            dma((NC, 2)), dma((NC, 2)),
            dma((NC, 4)), dma((NC, 4)),
            dma((NC, 3)), dma((NC, 3)),
        ],
        compiler_params=pltpu.CompilerParams(
            collective_id=0, has_side_effects=True, vmem_limit_bytes=56 * 1024 * 1024),
        cost_estimate=pl.CostEstimate(
            flops=6 * total * d * ff, bytes_accessed=6 * d * ff, transcendentals=total * ff),
    )(relay, tokens, expert_ids, gates, w_gate, w_up, w_down)


def solution(mesh):
    experts = mesh.shape["expert"]
    fits = mesh.shape["dp"] == 1 and experts == 16
    return jax.shard_map(
        functools.partial(fused, experts) if fits else body,
        mesh=mesh,
        in_specs=(
            P(("parts", "expert", "dp"), None),
            P(("parts", "expert")),
            P(("parts", "expert"), None),
            P(("parts", "expert"), None),
            P("expert", None, "dp"),
            P("expert", None, "dp"),
            P("expert", "dp", None),
        ),
        out_specs=P(("parts", "expert"), "dp"),
        check_vma=False,
    )
```

```python
import functools

import jax
import jax.numpy as jnp
from jax import lax
from jax.experimental import pallas as pl
from jax.experimental.pallas import tpu as pltpu
from jax.sharding import PartitionSpec as P


def slot_limit(block, top, experts):
    return min(block, max(2, 2 * block * top // experts))


def expert_part(moe_all, ids_all, gates_all, w_gate, w_up, w_down, block):
    rows = moe_all.shape[0]
    experts = lax.axis_size("expert")
    top = ids_all.shape[1]
    capacity = min(rows, slot_limit(block, top, experts) * experts)
    index = lax.axis_index("expert")
    hit = ids_all == index
    gate_f = gates_all.astype(jnp.float32)
    marked = jnp.any(hit, axis=1).astype(jnp.int32)
    weight = jnp.sum(jnp.where(hit, gate_f, jnp.zeros_like(gate_f)), axis=1)
    order = jnp.argsort(1 - marked, stable=True)[:capacity]
    picked = moe_all[order]
    gate_val = jnp.dot(picked, w_gate[0], preferred_element_type=jnp.float32)
    up_val = jnp.dot(picked, w_up[0], preferred_element_type=jnp.float32)
    hidden = (jax.nn.silu(gate_val) * up_val).astype(jnp.bfloat16)
    output = jnp.dot(hidden, w_down[0], preferred_element_type=jnp.float32)
    valid = marked[order]
    scale = weight[order] * valid.astype(jnp.float32)
    return (order, valid, marked, output * scale[:, None])


def body(tokens, relay, expert_ids, gates, w_gate, w_up, w_down):
    side = lax.axis_index("dp")
    block = relay.shape[0]
    block_rows = lax.all_gather(tokens, "dp", axis=0, tiled=True)
    local_rows = block_rows[relay]
    moe_all, ids_all, gates_all = (
        lax.all_gather(local_rows, "expert", axis=0, tiled=True),
        lax.all_gather(expert_ids, "expert", axis=0, tiled=True),
        lax.all_gather(gates, "expert", axis=0, tiled=True),
    )
    order, valid, marked, scaled = expert_part(
        moe_all, ids_all, gates_all, w_gate, w_up, w_down, block
    )
    rows = moe_all.shape[0]
    width = tokens.shape[1] // lax.axis_size("dp")
    partial_sum = jnp.zeros((rows, moe_all.shape[1]), jnp.float32).at[order].add(scaled)
    total = lax.psum(partial_sum, ("expert", "dp"))
    row_start = lax.axis_index("expert") * block
    col_start = side * width
    result = lax.dynamic_slice(total, (row_start, col_start), (block, width))
    return result.astype(jnp.bfloat16)


KC = 2
NC = 2
LANES = 128


def fused_kernel(relay_ref, tok_ref, ids_ref, gates_ref, wg_hbm, wu_hbm, wd_hbm, out_ref,
                 wg, wu, wd, acc_g, acc_u, g_bufs, f_bufs, c_out, c_in, x_out, x_in, z_out, z_in,
                 w_sem, zs, zr, xs, xr, cs, cr, rcs, rcr, rxs, rxr, rzs, rzr):
    f32, bf16 = jnp.float32, jnp.bfloat16
    rows, d = tok_ref.shape
    ff = wg.shape[1]
    total = 16 * rows
    kw, nw = d // KC, d // NC
    me = lax.axis_index("expert")
    c, x, z = lax.rem(me, 2), lax.rem(me // 2, 2), me // 4
    oc, ox = 1 - c, 1 - x

    def dev(zz, xx, cc):
        return {"expert": zz * 4 + xx * 2 + cc}

    h, l = z // 2, lax.rem(z, 2)
    oh, ol = 1 - h, 1 - l
    sib, across = dev(z, x, oc), dev(lax.rem(z + 2, 4), x, c)
    spots = ((x, ol), (ox, l), (ox, ol))
    near = [dev(2 * h + ll, xx, c) for xx, ll in spots]
    barrier = pltpu.get_barrier_semaphore()
    partners = [sib, across] + near
    for partner in partners:
        pl.semaphore_signal(barrier, inc=1, device_id=partner, device_id_type=pl.DeviceIdType.MESH)

    w_copies = []
    for k in range(KC):
        part = pl.ds(k * kw, kw)
        w_copies.append((
            pltpu.make_async_copy(wg_hbm.at[0, part], wg.at[part], w_sem.at[0, k]),
            pltpu.make_async_copy(wu_hbm.at[0, part], wu.at[part], w_sem.at[1, k]),
        ))
    d_copies = [
        pltpu.make_async_copy(wd_hbm.at[0, :, pl.ds(j * nw, nw)], wd.at[j], w_sem.at[2, j])
        for j in range(NC)
    ]
    for pair in w_copies:
        for copy in pair:
            copy.start()
    for copy in d_copies:
        copy.start()

    sub = lax.broadcasted_iota(jnp.int32, (rows, rows), 0)
    lane = lax.broadcasted_iota(jnp.int32, (rows, rows), 1)
    source = jnp.zeros((rows, rows), jnp.int32)
    for r in range(rows):
        source = jnp.where(sub == r, relay_ref[r], source)
    pick = jnp.where(source == lane, 1.0, 0.0).astype(bf16)
    wide = lax.broadcasted_iota(jnp.int32, (rows, LANES), 1)
    dense = jnp.zeros((rows, LANES), f32)
    ids = ids_ref[...]
    gates = gates_ref[...].astype(f32)
    for t in range(ids_ref.shape[1]):
        dense = dense + jnp.where(ids[:, t:t + 1] == wide, gates[:, t:t + 1], 0.0)
    for k in range(KC):
        moved = jnp.dot(pick, tok_ref[:, k * kw:(k + 1) * kw], preferred_element_type=f32)
        g_bufs[k][c, h, x, l, :, 0:kw] = moved.astype(bf16)
    g_bufs[0][c, h, x, l, :, kw:kw + LANES] = dense.astype(bf16)

    pl.semaphore_wait(barrier, len(partners))

    sent = []

    def send(src, dst, ss, rs, to):
        copy = pltpu.make_async_remote_copy(
            src_ref=src, dst_ref=dst, send_sem=ss, recv_sem=rs,
            device_id=to, device_id_type=pl.DeviceIdType.MESH)
        copy.start()
        sent.append(copy)

    def arrived(dst, ss, rs, to):
        pltpu.make_async_remote_copy(
            src_ref=dst, dst_ref=dst, send_sem=ss, recv_sem=rs,
            device_id=to, device_id_type=pl.DeviceIdType.MESH).wait_recv()

    def begin_far(k):
        block = g_bufs[k].at[c, h, x, l]
        send(block, block, zs.at[k, 3], zr.at[k, 3], across)

    def begin_near(k):
        block = g_bufs[k].at[c, h, x, l]
        for p in range(3):
            send(block, block, zs.at[k, p], zr.at[k, p], near[p])

    def forward(k):
        block = g_bufs[k].at[c, oh, x, l]
        arrived(block, zs.at[k, 3], zr.at[k, 3], across)
        for p in range(3):
            send(block, block, xs.at[k, p], xr.at[k, p], near[p])

    def share_near(k):
        g = g_bufs[k]
        for p, (xx, ll) in enumerate(spots):
            arrived(g.at[c, h, xx, ll], zs.at[k, p], zr.at[k, p], near[p])
        send(g.at[c, h], g.at[c, h], cs.at[k, 0], cr.at[k, 0], sib)

    def share_far(k):
        g = g_bufs[k]
        for p, (xx, ll) in enumerate(spots):
            arrived(g.at[c, oh, xx, ll], xs.at[k, p], xr.at[k, p], near[p])
        send(g.at[c, oh], g.at[c, oh], cs.at[k, 1], cr.at[k, 1], sib)

    def multiply(k):
        g = g_bufs[k]
        arrived(g.at[oc, h], cs.at[k, 0], cr.at[k, 0], sib)
        arrived(g.at[oc, oh], cs.at[k, 1], cr.at[k, 1], sib)
        a = g[:, :, :, :, :, 0:kw].reshape(total, kw)
        for copy, w, acc in zip(w_copies[k], (wg, wu), (acc_g, acc_u)):
            copy.wait()
            part = jnp.dot(a, w[k * kw:(k + 1) * kw, :], preferred_element_type=f32)
            if k == 0:
                acc[...] = part
            else:
                acc[...] += part

    for k in range(KC):
        begin_far(k)
        begin_near(k)
    for k in range(KC):
        forward(k)
        share_near(k)
    for k in range(KC):
        share_far(k)
        multiply(k)

    weights = g_bufs[0][:, :, :, :, :, kw:kw + LANES].reshape(total, LANES).astype(f32)
    mine = lax.broadcasted_iota(jnp.int32, (total, LANES), 1) == me
    weight = jnp.sum(jnp.where(mine, weights, 0.0), axis=1, keepdims=True)
    gate = acc_g[...]
    hidden = (gate / (1.0 + jnp.exp(-gate)) * acc_u[...]).astype(bf16)

    def down(j):
        f = f_bufs[j]
        d_copies[j].wait()
        part = jnp.dot(hidden, wd[j], preferred_element_type=f32) * weight
        f[...] = part.reshape(f.shape)
        for q, hh in enumerate((oh, h)):
            c_out[j, hh] = f[oc, hh].astype(bf16)
            send(c_out.at[j, hh], c_in.at[j, hh], rcs.at[j, q], rcr.at[j, q], sib)

    def both(j, hh, xx, ll):
        return f_bufs[j][c, hh, xx, ll] + c_in[j, hh, xx, ll].astype(f32)

    def out_far(j):
        arrived(c_in.at[j, oh], rcs.at[j, 0], rcr.at[j, 0], sib)
        for p, (xx, ll) in enumerate(spots):
            x_out[j, p] = both(j, oh, xx, ll).astype(bf16)
            send(x_out.at[j, p], x_in.at[j, p], rxs.at[j, p], rxr.at[j, p], near[p])

    def out_near(j):
        arrived(c_in.at[j, h], rcs.at[j, 1], rcr.at[j, 1], sib)
        for p, (xx, ll) in enumerate(spots):
            z_out[j, p] = both(j, h, xx, ll).astype(bf16)
            send(z_out.at[j, p], z_in.at[j, p], rzs.at[j, p], rzr.at[j, p], near[p])

    def cross(j):
        t = both(j, oh, x, l)
        for p in range(3):
            arrived(x_in.at[j, p], rxs.at[j, p], rxr.at[j, p], near[p])
            t = t + x_in[j, p].astype(f32)
        x_out[j, 3] = t.astype(bf16)
        send(x_out.at[j, 3], x_in.at[j, 3], rxs.at[j, 3], rxr.at[j, 3], across)

    def finish(j):
        t = both(j, h, x, l)
        for p in range(3):
            arrived(z_in.at[j, p], rzs.at[j, p], rzr.at[j, p], near[p])
            t = t + z_in[j, p].astype(f32)
        arrived(x_in.at[j, 3], rxs.at[j, 3], rxr.at[j, 3], across)
        t = t + x_in[j, 3].astype(f32)
        out_ref[:, j * nw:(j + 1) * nw] = t.astype(bf16)

    for j in range(NC):
        down(j)
        out_far(j)
    for j in range(NC):
        out_near(j)
        cross(j)
    for j in range(NC):
        finish(j)

    for copy in sent:
        copy.wait_send()


def fused(experts, tokens, relay, expert_ids, gates, w_gate, w_up, w_down):
    rows, d = tokens.shape
    ff = w_gate.shape[2]
    kw, nw = d // KC, d // NC
    bf16, f32 = jnp.bfloat16, jnp.float32
    vmem = pl.BlockSpec(memory_space=pltpu.VMEM)
    hbm = pl.BlockSpec(memory_space=pl.ANY)
    dma = pltpu.SemaphoreType.DMA
    total = experts * rows
    return pl.pallas_call(
        fused_kernel,
        out_shape=jax.ShapeDtypeStruct((rows, d), bf16),
        in_specs=[pl.BlockSpec(memory_space=pltpu.SMEM), vmem, vmem, vmem, hbm, hbm, hbm],
        out_specs=vmem,
        scratch_shapes=[
            pltpu.VMEM((d, ff), bf16),
            pltpu.VMEM((d, ff), bf16),
            pltpu.VMEM((NC, ff, nw), bf16),
            pltpu.VMEM((total, ff), f32),
            pltpu.VMEM((total, ff), f32),
            [pltpu.VMEM((2, 2, 2, 2, rows, kw + (LANES if k == 0 else 0)), bf16) for k in range(KC)],
            [pltpu.VMEM((2, 2, 2, 2, rows, nw), f32) for j in range(NC)],
            pltpu.VMEM((NC, 2, 2, 2, rows, nw), bf16),
            pltpu.VMEM((NC, 2, 2, 2, rows, nw), bf16),
            pltpu.VMEM((NC, 4, rows, nw), bf16),
            pltpu.VMEM((NC, 4, rows, nw), bf16),
            pltpu.VMEM((NC, 3, rows, nw), bf16),
            pltpu.VMEM((NC, 3, rows, nw), bf16),
            dma((3, max(KC, NC))),
            dma((KC, 4)), dma((KC, 4)),
            dma((KC, 3)), dma((KC, 3)),
            dma((KC, 2)), dma((KC, 2)),
            dma((NC, 2)), dma((NC, 2)),
            dma((NC, 4)), dma((NC, 4)),
            dma((NC, 3)), dma((NC, 3)),
        ],
        compiler_params=pltpu.CompilerParams(
            collective_id=0, has_side_effects=True, vmem_limit_bytes=56 * 1024 * 1024),
        cost_estimate=pl.CostEstimate(
            flops=6 * total * d * ff, bytes_accessed=6 * d * ff, transcendentals=total * ff),
    )(relay, tokens, expert_ids, gates, w_gate, w_up, w_down)


def solution(mesh):
    experts = mesh.shape["expert"]
    fits = mesh.shape["dp"] == 1 and experts == 16
    return jax.shard_map(
        functools.partial(fused, experts) if fits else body,
        mesh=mesh,
        in_specs=(
            P(("parts", "expert", "dp"), None),
            P(("parts", "expert")),
            P(("parts", "expert"), None),
            P(("parts", "expert"), None),
            P("expert", None, "dp"),
            P("expert", None, "dp"),
            P("expert", "dp", None),
        ),
        out_specs=P(("parts", "expert"), "dp"),
        check_vma=False,
    )
```
